256 devices in a mesh: wide: 32 (over x, z), narrow: 8 (over y, core).
Axes of the slice: x: 4, y: 4, z: 8, core: 2. Of those that a mesh axis runs over, the one named last changes fastest.
Arguments:
- residual: bfloat16 [256, 768, 1024], P(('wide', 'narrow')), may hold values from -6 to 6
- share: bfloat16 [256, 1024], P(('wide', 'narrow')), may hold values from 0.19921875 to 0.796875
- orient: int32 [256, 2, 512], P(('wide', 'narrow')), may hold values from 0 to 511, each once within a row
- local_inverse: bfloat16 [256, 2048, 2048], P(('wide', 'narrow')), may hold values from -2 to 5, as said below
- primal_basis: bfloat16 [256, 24, 2048], P(('wide', 'narrow')), may hold values from -0.29882812 to 0.29882812
- primal_index: int32 [256, 24], replicated, may hold values from 0 to 2303
- coarse_inverse: float32 [2304, 2304], P(('wide', 'narrow')), may hold values from -1 to 4, as said below
Outputs:
- assembled: bfloat16 [256, 768, 1024], P(('wide', 'narrow'))
The draws below stay inside these ranges and needn't reach their ends.
Inputs may be any that keep to these rules, and one draw needn't show every extreme that they name: `orient`: each row is a permutation of 0 to 511. `local_inverse`: each patch's matrix is symmetric positive definite. `coarse_inverse`: symmetric positive definite.
All inputs are finite; a program needn't handle non-finite values.
Results may differ from the reference program's by a relative error of at most 0.0056.
Values may be sent and summed in bfloat16 or wider, within the bound.
No kernel may reach another device: no remote copies, remote signals or barrier semaphores. Data moves between devices by JAX's collectives and lax.ppermute only.
A program may use at most 128 MiB of HBM per device.

```python
import jax
import jax.numpy as jnp
from jax import lax

W = 2048
R = 768
NPRIM = 24
FACE = 512
NPATCH = 256
NC = 2304
N_WIDE = 32
N_NARROW = 8


def draw_local_inverse(key, part):
    key = jax.random.fold_in(key, 11)
    keys = jax.random.split(key, NPATCH)
    scale = (2.0 * W) ** (-0.5)

    def one_patch(sub):
        key_off, key_diag = jax.random.split(sub)
        noise = jax.random.normal(key_off, (W, W), jnp.float32)
        diag_vals = jax.random.uniform(key_diag, (W,), jnp.float32, 2.5, 3.5)
        matrix = (noise + noise.T) * scale + jnp.eye(W, dtype=jnp.float32) * diag_vals[None, :]
        return matrix.astype(jnp.bfloat16)
    return lax.map(one_patch, keys)


def draw_coarse_inverse(key, part):
    key = jax.random.fold_in(key, 23)
    key_off, key_diag = jax.random.split(key)
    scale = (2.0 * NC) ** (-0.5)
    noise = jax.random.normal(key_off, (NC, NC), jnp.float32)
    diag_vals = jax.random.uniform(key_diag, (NC,), jnp.float32, 2.5, 3.5)
    return (noise + noise.T) * scale + jnp.eye(NC, dtype=jnp.float32) * diag_vals[None, :]


def plant(values, rng, low, top_value):
    place = [jax.random.randint(jax.random.fold_in(rng, axis), (), 0, length) for axis, length in enumerate(values.shape)]
    widest = values.shape.index(max(values.shape))
    beside = place[:widest] + [(place[widest] + 1) % values.shape[widest]] + place[widest + 1:]
    return values.at[tuple(place)].set(low).at[tuple(beside)].set(top_value)


def level_of(own_key, extent, cuts, low, largest):
    factor_of, own = 1.0, jax.random.fold_in(own_key, 6)
    for axis_at, blocks in cuts:
        draws = jnp.exp(jax.random.uniform(jax.random.fold_in(own, axis_at), (blocks,), jnp.float32, low / len(cuts), largest / len(cuts)))
        factor_of = factor_of * jnp.repeat(draws, extent[axis_at] // blocks).reshape([-1 if axis == axis_at else 1 for axis in range(len(extent))])
    return factor_of


def scatter_about(stream_key, extent, scale, bound, cuts=(), held_as=jnp.bfloat16):
    drawn = jax.random.normal(stream_key, extent, jnp.float32) * scale
    if len(cuts) > 0:
        drawn = level_of(stream_key, extent, cuts, -0.22, 0.18) * drawn
    return jnp.clip(drawn, min=-bound, max=bound).astype(held_as)


def setup_inputs(seed: int = 0) -> dict:
    splits = jax.random.split(jax.random.key(seed), 8)
    return {
        "residual": scatter_about(splits[0], (NPATCH, R, 2 * FACE), 1.0, 6.0, ((0, 256),)),
        "share": jnp.clip(0.19921875 + 0.59765625 * jax.random.uniform(splits[1], (NPATCH, 2 * FACE), jnp.float32) ** level_of(splits[1], (NPATCH, 2 * FACE), ((0, 256),), -0.2, 0.2), 0.19921875, 0.796875).astype(jnp.bfloat16),
        "orient": jax.vmap(lambda own: jax.random.permutation(own, FACE))(jax.random.split(splits[2], NPATCH * 2)).reshape((NPATCH, 2, FACE)).astype(jnp.int32),
        "local_inverse": draw_local_inverse(jax.random.fold_in(splits[7], 71), 0),
        "primal_basis": scatter_about(splits[4], (NPATCH, NPRIM, W), 0.05, 0.29882812, ((0, 256),)),
        "primal_index": plant(jax.random.randint(splits[5], (NPATCH, NPRIM), 0, NC), jax.random.fold_in(splits[5], 1), 0, NC - 1).astype(jnp.int32),
        "coarse_inverse": draw_coarse_inverse(jax.random.fold_in(splits[7], 71), 0),
    }


def reference(residual, share, orient, local_inverse, primal_basis, primal_index, coarse_inverse):
    nwide = N_WIDE
    nnar = N_NARROW
    face = FACE
    res = residual.reshape(nwide, nnar, R, 2 * face)
    shr = share.reshape(nwide, nnar, 2 * face).astype(jnp.float32)
    ori = orient.reshape(nwide, nnar, 2, face).astype(jnp.int32)
    res_wide = jnp.roll(res[..., :face], 1, axis=0)
    res_nar = jnp.roll(res[..., face:], 1, axis=1)
    shr_wide = jnp.roll(shr[..., :face], 1, axis=0)
    shr_nar = jnp.roll(shr[..., face:], 1, axis=1)
    idx_wide = jnp.broadcast_to(ori[:, :, None, 0, :], (nwide, nnar, R, face))
    idx_nar = jnp.broadcast_to(ori[:, :, None, 1, :], (nwide, nnar, R, face))
    got_wide = jnp.take_along_axis(res_wide, idx_wide, axis=3)
    got_nar = jnp.take_along_axis(res_nar, idx_nar, axis=3)
    wt_wide = jnp.take_along_axis(shr_wide, ori[:, :, 0, :], axis=2)
    wt_nar = jnp.take_along_axis(shr_nar, ori[:, :, 1, :], axis=2)
    weights = jnp.concatenate([shr, 1.0 - wt_wide, 1.0 - wt_nar], axis=-1)
    values = jnp.concatenate([res, got_wide, got_nar], axis=-1)
    gathered = (weights[:, :, None, :] * values.astype(jnp.float32)).astype(jnp.bfloat16)
    gathered = gathered.reshape(NPATCH, R, W)
    weights = weights.reshape(NPATCH, W)

    def primal_one(pair):
        return jnp.dot(pair[0], pair[1].T, preferred_element_type=jnp.float32)

    primal = lax.map(primal_one, (gathered, primal_basis))
    flat_vals = jnp.transpose(primal, (1, 0, 2)).reshape(R, NPATCH * NPRIM)
    coarse_rhs = jnp.zeros((R, NC), jnp.float32).at[:, primal_index.reshape(-1)].add(flat_vals)
    coarse_corr = jnp.dot(coarse_rhs, coarse_inverse.T, precision=lax.Precision.HIGHEST)
    patch_corr = jnp.transpose(coarse_corr[:, primal_index], (1, 0, 2))

    def apply_one(items):
        block, inverse, basis, corr, weight = items
        local = jnp.dot(block, inverse, preferred_element_type=jnp.float32)
        coarse = jnp.dot(corr, basis.astype(jnp.float32), precision=lax.Precision.HIGHEST)
        return (weight[None, :] * (local + coarse)).astype(jnp.bfloat16)

    weighted = lax.map(apply_one, (gathered, local_inverse, primal_basis, patch_corr, weights))
    weighted = weighted.reshape(nwide, nnar, R, W)
    inverse_ori = jnp.argsort(ori, axis=-1).astype(jnp.int32)
    inv_wide = jnp.broadcast_to(inverse_ori[:, :, None, 0, :], (nwide, nnar, R, face))
    inv_nar = jnp.broadcast_to(inverse_ori[:, :, None, 1, :], (nwide, nnar, R, face))
    sent_wide = jnp.take_along_axis(weighted[..., 2 * face:3 * face], inv_wide, axis=3)
    sent_nar = jnp.take_along_axis(weighted[..., 3 * face:], inv_nar, axis=3)
    back_wide = jnp.roll(sent_wide, -1, axis=0).astype(jnp.float32)
    back_nar = jnp.roll(sent_nar, -1, axis=1).astype(jnp.float32)
    own = weighted[..., :2 * face].astype(jnp.float32)
    total = own + jnp.concatenate([back_wide, back_nar], axis=-1)
    return total.astype(jnp.bfloat16).reshape(NPATCH, R, 2 * face)
```

```python
import jax
import jax.numpy as jnp
from jax import lax
from jax.experimental import pallas as pl
from jax.experimental.pallas import tpu as pltpu
from jax.sharding import PartitionSpec as P

BF = jnp.bfloat16
F32 = jnp.float32
NX = 4
NZ = 8
NY = 4
NCORE = 2
NARROW = NY * NCORE
WIDE = NX * NZ
WIDE_AXES = ("x", "z")
NARROW_AXES = ("y", "core")
LANES = 128
SLOT = 32
NT = (((1,), (1,)), ((), ()))
MIB = 1024 * 1024


def permute(array, axes, target):
    count = lax.axis_size(axes)
    return lax.ppermute(array, axes, [(i, target(i)) for i in range(count)])


def shift(array, axes, by):
    count = lax.axis_size(axes)
    return permute(array, axes, lambda i: (i + by) % count)


def exchange(array, bit):
    return permute(array, "z", lambda i: i ^ bit)


def whole(shape):
    return pl.BlockSpec(shape, lambda *_: (0,) * len(shape))


def params(mib=8):
    return pltpu.CompilerParams(vmem_limit_bytes=mib * MIB)


def after(array, *others):
    return lax.optimization_barrier((array, *others))[0]


def one_hot(row, count):
    lanes = row.shape[1]
    return jnp.where(lax.broadcasted_iota(jnp.int32, (count, lanes), 0) == row, 1.0, 0.0).astype(BF)


def dot_nt(a, b):
    return lax.dot_general(a, b, NT, preferred_element_type=F32)


def padded(basis):
    fill = jnp.zeros((SLOT - basis.shape[0], basis.shape[1]), F32)
    return jnp.concatenate([basis.astype(F32), fill], axis=0).astype(BF)


def cost(flops, moved):
    return pl.CostEstimate(flops=flops, bytes_accessed=moved, transcendentals=0)


def fetch(pairs, sems):
    copies = [pltpu.make_async_copy(src, dst, sems.at[i]) for i, (src, dst) in enumerate(pairs)]
    for copy in copies:
        copy.start()
    return copies


IN_HBM = pl.BlockSpec(memory_space=pltpu.HBM)


def first_kernel(
    basis_hbm, orient_hbm, coarse_hbm, wide_ref, narrow_ref, lines_ref, basis_ref, orient_ref, coarse_ref, strided, sems
):
    copies = fetch(((basis_hbm, basis_ref), (orient_hbm, orient_ref), (coarse_hbm, coarse_ref)), sems)
    copies[0].wait()
    copies[1].wait()
    face = orient_ref.shape[1]
    for row, out in ((0, wide_ref), (1, narrow_ref)):
        order = one_hot(orient_ref[row : row + 1, :], face)
        part = padded(basis_ref[:, (2 + row) * face : (3 + row) * face])
        out[...] = dot_nt(part, order).astype(BF)
    held, coarse = coarse_ref.shape
    blocks = coarse // LANES
    strided[...] = jnp.zeros_like(strided)
    copies[2].wait()
    for b in range(blocks):
        strided[pl.ds(b, held, stride=blocks), :] = coarse_ref[:, b * LANES : (b + 1) * LANES]
    lines_ref[...] = strided[: lines_ref.shape[0]].astype(BF)


def line_count(held, coarse):
    return -(-held * coarse // LANES // 16) * 16


def first(basis, orient, coarse_inverse):
    face = orient.shape[1]
    shape = jax.ShapeDtypeStruct((SLOT, face), BF)
    lines = (line_count(*coarse_inverse.shape), LANES)
    inputs = (basis, orient, coarse_inverse)
    return pl.pallas_call(
        first_kernel,
        in_specs=[IN_HBM] * len(inputs),
        out_shape=[shape, shape, jax.ShapeDtypeStruct(lines, BF)],
        scratch_shapes=[pltpu.VMEM(a.shape, a.dtype) for a in inputs]
        + [pltpu.VMEM((2 * lines[0], LANES), F32), pltpu.SemaphoreType.DMA((len(inputs),))],
        compiler_params=params(60),
    )(*inputs)


def outgoing_kernel(res_ref, share_ref, face_wide_ref, face_narrow_ref):
    face = face_wide_ref.shape[1]
    given = res_ref[...].astype(F32) * (1.0 - share_ref[...].astype(F32))
    face_wide_ref[...] = given[:, :face].astype(BF)
    face_narrow_ref[...] = given[:, face:].astype(BF)


def outgoing(res, share):
    rows, owned_count = res.shape
    face = owned_count // 2
    block = rows // 3
    half = jax.ShapeDtypeStruct((rows, face), BF)
    by_rows = lambda i: (i, 0)
    return pl.pallas_call(
        outgoing_kernel,
        grid=(3,),
        in_specs=[pl.BlockSpec((block, owned_count), by_rows), whole(share.shape)],
        out_specs=[pl.BlockSpec((block, face), by_rows)] * 2,
        out_shape=[half, half],
        compiler_params=params(),
        cost_estimate=cost(2 * res.size, 4 * res.size),
    )(res, share)


def stacked_bases(own_ref, wide_ref, narrow_ref):
    face = wide_ref.shape[1]
    zero = jnp.zeros((SLOT, face), BF)
    zeros = jnp.zeros((SLOT, 2 * face), BF)
    mine = jnp.concatenate([padded(own_ref[:, : 2 * face]), zeros, zeros, zeros], axis=0)
    theirs = jnp.concatenate(
        [
            zeros,
            jnp.concatenate([wide_ref[...], zero], axis=1),
            jnp.concatenate([zero, narrow_ref[...]], axis=1),
            zeros,
        ],
        axis=0,
    )
    return mine, theirs


def primal_kernel(res_ref, share_ref, own_ref, wide_ref, narrow_ref, out_ref):
    mine, theirs = stacked_bases(own_ref, wide_ref, narrow_ref)
    res = res_ref[...].astype(F32)
    shr = share_ref[...].astype(F32)
    kept = (res * shr).astype(BF)
    given = (res * (1.0 - shr)).astype(BF)
    out_ref[...] = (dot_nt(kept, mine) + dot_nt(given, theirs)).astype(BF)


def primal_parts(res, share, basis, basis_wide, basis_narrow):
    rows, owned_count = res.shape
    block = rows // 3
    return pl.pallas_call(
        primal_kernel,
        grid=(3,),
        in_specs=[
            pl.BlockSpec((block, owned_count), lambda i: (i, 0)),
            whole(share.shape),
            whole(basis.shape),
            whole(basis_wide.shape),
            whole(basis_narrow.shape),
        ],
        out_specs=pl.BlockSpec((block, LANES), lambda i: (i, 0)),
        out_shape=jax.ShapeDtypeStruct((rows, LANES), BF),
        compiler_params=params(16),
        cost_estimate=cost(4 * res.size * LANES, 2 * res.size),
    )(res, share, basis, basis_wide, basis_narrow)


def scatter_kernel(blocks, x_ref, high_ref, low_ref, out_ref, masked):
    rows = x_ref.shape[1]
    masked[...] = jnp.zeros_like(masked)
    total = jnp.zeros((blocks * SLOT, LANES), F32)
    for pair in range(x_ref.shape[0] // 2):
        x = jnp.concatenate([x_ref[2 * pair], x_ref[2 * pair + 1]], axis=1).astype(F32)
        high = jnp.concatenate([high_ref[2 * pair : 2 * pair + 1], high_ref[2 * pair + 1 : 2 * pair + 2]], axis=1)
        low = jnp.concatenate([low_ref[2 * pair : 2 * pair + 1], low_ref[2 * pair + 1 : 2 * pair + 2]], axis=1)
        x = jnp.concatenate([x, jnp.zeros((SLOT - rows, x.shape[1]), F32)], axis=0)
        for b in range(blocks):
            masked[b * SLOT : (b + 1) * SLOT] = jnp.where(high == b, x, 0.0).astype(BF)
        total += dot_nt(masked[...], one_hot(low, LANES))
    for b in range(blocks):
        out_ref[b] = total[b * SLOT : b * SLOT + rows].astype(BF)


def scatter(x, high, low, blocks):
    _, rows, _ = x.shape
    return pl.pallas_call(
        lambda *refs: scatter_kernel(blocks, *refs),
        out_shape=jax.ShapeDtypeStruct((blocks, rows, LANES), BF),
        scratch_shapes=[pltpu.VMEM((blocks * SLOT, 2 * LANES), BF)],
        compiler_params=params(),
    )(x, high, low)


def solve_kernel(parts_ref, *refs):
    *line_refs, out_ref, strided, inverse = refs
    parts, blocks, rows, _ = parts_ref.shape
    count = line_refs[0].shape[0]
    size = count // NZ
    strided[count:] = jnp.zeros((strided.shape[0] - count, LANES), F32)
    for x, ref in enumerate(line_refs):
        strided[:count] = ref[...].astype(F32)
        for z in range(NZ):
            at = x * LANES + z * 16
            for b in range(blocks):
                found = strided[pl.ds(z * size + b, 16, stride=blocks), :]
                inverse[at : at + 16, b * LANES : (b + 1) * LANES] = found.astype(BF)
    total = jnp.concatenate([sum(parts_ref[p, b].astype(F32) for p in range(parts)) for b in range(blocks)], axis=1)
    top = total.astype(BF)
    rest = (total - top.astype(F32)).astype(BF)
    both = jnp.concatenate([top.astype(F32), rest.astype(F32)], axis=0).astype(BF)
    product = dot_nt(both, inverse[...])
    product = (product[:rows] + product[rows:]).astype(BF)
    for p in range(NX):
        for n in range(out_ref.shape[0]):
            out_ref[n, p] = product[:, p * LANES : (p + 1) * LANES]


def solve(parts, lines):
    _, blocks, rows, _ = parts.shape
    spare = 16 * blocks
    return pl.pallas_call(
        solve_kernel,
        out_shape=jax.ShapeDtypeStruct((NARROW, NX, rows, LANES), BF),
        scratch_shapes=[
            pltpu.VMEM((lines[0].shape[0] + spare, LANES), F32),
            pltpu.VMEM((NX * LANES, blocks * LANES), BF),
        ],
        compiler_params=params(16),
    )(parts, *lines)


def gather_kernel(rows, corr_ref, high_ref, low_ref, out_ref):
    blocks = corr_ref.shape[0] // rows
    for pair in range(out_ref.shape[0] // 2):
        high = jnp.concatenate([high_ref[2 * pair : 2 * pair + 1], high_ref[2 * pair + 1 : 2 * pair + 2]], axis=1)
        low = jnp.concatenate([low_ref[2 * pair : 2 * pair + 1], low_ref[2 * pair + 1 : 2 * pair + 2]], axis=1)
        found = jnp.dot(corr_ref[...], one_hot(low, LANES), preferred_element_type=F32)
        total = jnp.zeros((rows, 2 * LANES), F32)
        for b in range(blocks):
            total = jnp.where(high == b, found[b * rows : (b + 1) * rows], total)
        out_ref[2 * pair] = total[:, :LANES].astype(BF)
        out_ref[2 * pair + 1] = total[:, LANES:].astype(BF)


def gather(corr, high, low, rows):
    return pl.pallas_call(
        lambda *refs: gather_kernel(rows, *refs),
        out_shape=jax.ShapeDtypeStruct((high.shape[0], rows, LANES), BF),
        compiler_params=params(),
    )(corr, high, low)


def column_copies(inverse_hbm, inverse, sems, first_column):
    count, rows, width = inverse.shape
    return [
        pltpu.make_async_copy(
            inverse_hbm.at[pl.ds(0, rows), pl.ds((first_column + i) * width, width)], inverse.at[i], sems.at[i]
        )
        for i in range(count)
    ]


def faces_kernel(
    res_ref, share_ref, got_wide_ref, got_narrow_ref, orient_ref, inverse_hbm, gathered_ref, wide_ref, narrow_ref, inverse, sems
):
    face = orient_ref.shape[1]
    copies = column_copies(inverse_hbm, inverse, sems, 2)
    for copy in copies:
        copy.start()
    gathered_ref[:, : 2 * face] = (res_ref[...].astype(F32) * share_ref[...].astype(F32)).astype(BF)
    orders = [one_hot(orient_ref[row : row + 1, :], face) for row in (0, 1)]
    for row, ref in ((0, got_wide_ref), (1, got_narrow_ref)):
        found = jnp.dot(ref[...], orders[row], preferred_element_type=F32)
        gathered_ref[:, (2 + row) * face : (3 + row) * face] = found.astype(BF)
    for row, ref in ((0, wide_ref), (1, narrow_ref)):
        copies[row].wait()
        product = jnp.dot(gathered_ref[...], inverse[row], preferred_element_type=F32).astype(BF)
        ref[...] = dot_nt(product, orders[row]).astype(BF)


def faces(res, share, got_wide, got_narrow, orient, inverse):
    rows = res.shape[0]
    face = orient.shape[1]
    unknowns = inverse.shape[0]
    half = jax.ShapeDtypeStruct((rows, face), BF)
    inputs = (res, share, got_wide, got_narrow, orient)
    return pl.pallas_call(
        faces_kernel,
        in_specs=[pl.BlockSpec(memory_space=pltpu.VMEM)] * len(inputs) + [IN_HBM],
        out_shape=[jax.ShapeDtypeStruct((rows, unknowns), BF), half, half],
        scratch_shapes=[pltpu.VMEM((2, unknowns, face), BF), pltpu.SemaphoreType.DMA((2,))],
        compiler_params=params(56),
        cost_estimate=cost(4 * rows * face * unknowns + 8 * rows * face * face, 4 * face * unknowns + 8 * rows * face),
    )(*inputs, inverse)


def owned_kernel(gathered_ref, inverse_hbm, out_ref, inverse, sems):
    copies = column_copies(inverse_hbm, inverse, sems, 0)
    face = inverse.shape[2]
    for copy in copies:
        copy.start()
    for i, copy in enumerate(copies):
        copy.wait()
        product = jnp.dot(gathered_ref[...], inverse[i], preferred_element_type=F32)
        out_ref[:, i * face : (i + 1) * face] = product.astype(BF)


def owned(gathered, inverse, face):
    rows, unknowns = gathered.shape
    return pl.pallas_call(
        owned_kernel,
        in_specs=[pl.BlockSpec(memory_space=pltpu.VMEM), IN_HBM],
        out_shape=jax.ShapeDtypeStruct((rows, 2 * face), BF),
        scratch_shapes=[pltpu.VMEM((2, unknowns, face), BF), pltpu.SemaphoreType.DMA((2,))],
        compiler_params=params(56),
        cost_estimate=cost(4 * rows * face * unknowns, 4 * face * unknowns + 4 * rows * unknowns),
    )(gathered, inverse)


def final_kernel(local_ref, back_wide_ref, back_narrow_ref, corr_ref, share_ref, own_ref, wide_ref, narrow_ref, out_ref):
    mine, theirs = stacked_bases(own_ref, wide_ref, narrow_ref)
    shr = share_ref[...].astype(F32)
    corr = corr_ref[...]
    kept = local_ref[...].astype(F32) + jnp.dot(corr, mine, preferred_element_type=F32)
    back = jnp.concatenate([back_wide_ref[...], back_narrow_ref[...]], axis=1).astype(F32)
    back = back + jnp.dot(corr, theirs, preferred_element_type=F32)
    out_ref[0] = (shr * kept + (1.0 - shr) * back).astype(BF)


def final(local, back_wide, back_narrow, corr, share, basis, basis_wide, basis_narrow):
    rows, owned_count = local.shape
    face = owned_count // 2
    block = rows // 3
    by_rows = lambda i: (i, 0)
    return pl.pallas_call(
        final_kernel,
        grid=(3,),
        in_specs=[
            pl.BlockSpec((block, owned_count), by_rows),
            pl.BlockSpec((block, face), by_rows),
            pl.BlockSpec((block, face), by_rows),
            pl.BlockSpec((block, LANES), by_rows),
            whole(share.shape),
            whole(basis.shape),
            whole(basis_wide.shape),
            whole(basis_narrow.shape),
        ],
        out_specs=pl.BlockSpec((1, block, owned_count), lambda i: (0, i, 0)),
        out_shape=jax.ShapeDtypeStruct((1, rows, owned_count), BF),
        compiler_params=params(12),
    )(local, back_wide, back_narrow, corr, share, basis, basis_wide, basis_narrow)


def patch_columns(primal_index):
    narrow = lax.axis_index(NARROW_AXES)
    count = primal_index.shape[1]
    grid = primal_index.reshape(WIDE, NARROW, count)
    grid = jnp.pad(grid, ((0, 0), (0, 0), (0, SLOT - count)), constant_values=-1)
    own = lax.dynamic_index_in_dim(grid, narrow, 1, keepdims=False)
    beside = lax.dynamic_index_in_dim(grid, (narrow + 1) % NARROW, 1, keepdims=False)
    empty = jnp.full((WIDE, LANES - 3 * SLOT), -1, jnp.int32)
    return jnp.concatenate([own, jnp.roll(own, -1, axis=0), beside, empty], axis=1)


def held_place(columns, held):
    owner, row = columns // held, columns % held
    w, n = owner // NARROW, owner % NARROW
    by_x = (lax.axis_index("x") - w // NZ) % NX
    apart = (lax.axis_index("z") ^ w) % NZ
    by_z = apart // 4 + (apart // 2) % 2 * 2 + apart % 2 * 4
    return jnp.where(columns < 0, -1, n * NX + by_x), by_z * 16 + row


def on_device(residual, share, orient, local_inverse, primal_basis, primal_index, coarse_inverse):
    res = residual[0]
    ori = orient[0]
    inverse = local_inverse[0]
    basis = primal_basis[0]
    rows = res.shape[0]
    held, coarse = coarse_inverse.shape
    chunk = rows // WIDE

    mine_wide, mine_narrow, lines = first(basis, ori, coarse_inverse)
    basis_wide = shift(mine_wide, WIDE_AXES, -1)
    basis_narrow = shift(mine_narrow, NARROW_AXES, -1)
    other = exchange(lines, 4)

    face_wide, face_narrow = outgoing(after(res, mine_wide), share)
    got_wide = shift(face_wide, WIDE_AXES, 1)
    got_narrow = shift(face_narrow, NARROW_AXES, 1)

    primal = primal_parts(after(res, face_wide), share, basis, basis_wide, basis_narrow)
    lines = jnp.concatenate([after(lines, primal), other], axis=0)
    other = exchange(lines, 2)
    chunks = lax.all_to_all(after(primal, lines).reshape(WIDE, chunk, LANES), WIDE_AXES, 0, 0)

    columns = patch_columns(after(primal_index, primal))
    high, low = columns >> 7, columns & 127
    high_held, low_held = held_place(columns, held)

    lines = jnp.concatenate([after(lines, high, high_held), other], axis=0)
    lines = jnp.concatenate([lines, exchange(lines, 1)], axis=0)
    pieces = [lines] + [shift(lines, "x", k) for k in range(1, NX)]

    partial = scatter(after(chunks, lines), high, low, coarse // LANES)
    parts = lax.all_gather(partial, NARROW_AXES)
    corr = solve(parts, pieces)

    gathered, send_wide, send_narrow = faces(res, share, after(got_wide, corr), got_narrow, ori, inverse)
    corr = lax.all_to_all(corr, NARROW_AXES, 0, 0)
    back_wide = shift(after(send_wide, corr), WIDE_AXES, -1)
    back_narrow = shift(after(send_narrow, corr), NARROW_AXES, -1)
    corr = gather(after(corr, send_wide).reshape(-1, LANES), high_held, low_held, chunk)
    local = owned(after(gathered, corr), inverse, face_wide.shape[1])
    corr = lax.all_to_all(corr, WIDE_AXES, 0, 0).reshape(rows, LANES)

    return final(local, back_wide, back_narrow, corr, share, basis, basis_wide, basis_narrow)


def solution(mesh):
    grid = jax.sharding.Mesh(mesh.devices.reshape(NX, NZ, NY, NCORE), WIDE_AXES + NARROW_AXES)
    patches = WIDE_AXES + NARROW_AXES
    placed = (
        P(patches, None, None),
        P(patches, None),
        P(patches, None, None),
        P(patches, None, None),
        P(patches, None, None),
        P(),
        P(patches, None),
    )
    return jax.shard_map(
        on_device,
        mesh=grid,
        in_specs=placed,
        out_specs=P(patches, None, None),
        check_vma=False,
    )
```

```python
import jax
import jax.numpy as jnp
from jax import lax
from jax.experimental import pallas as pl
from jax.experimental.pallas import tpu as pltpu
from jax.sharding import PartitionSpec as P

BF = jnp.bfloat16
F32 = jnp.float32
NX = 4
NZ = 8
NY = 4
NCORE = 2
NARROW = NY * NCORE
WIDE = NX * NZ
WIDE_AXES = ("x", "z")
NARROW_AXES = ("y", "core")
LANES = 128
SLOT = 32
NT = (((1,), (1,)), ((), ()))
MIB = 1024 * 1024


def permute(array, axes, target):
    count = lax.axis_size(axes)
    return lax.ppermute(array, axes, [(i, target(i)) for i in range(count)])


def shift(array, axes, by):
    count = lax.axis_size(axes)
    return permute(array, axes, lambda i: (i + by) % count)


def exchange(array, bit):
    return permute(array, "z", lambda i: i ^ bit)


def whole(shape):
    return pl.BlockSpec(shape, lambda *_: (0,) * len(shape))


def params(mib=8):
    return pltpu.CompilerParams(vmem_limit_bytes=mib * MIB)


def after(array, *others):
    return lax.optimization_barrier((array, *others))[0]


def one_hot(row, count):
    lanes = row.shape[1]
    return jnp.where(lax.broadcasted_iota(jnp.int32, (count, lanes), 0) == row, 1.0, 0.0).astype(BF)


def dot_nt(a, b):
    return lax.dot_general(a, b, NT, preferred_element_type=F32)


def padded(basis):
    fill = jnp.zeros((SLOT - basis.shape[0], basis.shape[1]), F32)
    return jnp.concatenate([basis.astype(F32), fill], axis=0).astype(BF)


def cost(flops, moved):
    return pl.CostEstimate(flops=flops, bytes_accessed=moved, transcendentals=0)


def fetch(pairs, sems):
    copies = [pltpu.make_async_copy(src, dst, sems.at[i]) for i, (src, dst) in enumerate(pairs)]
    for copy in copies:
        copy.start()
    return copies


IN_HBM = pl.BlockSpec(memory_space=pltpu.HBM)


def lines_kernel(coarse_hbm, lines_ref, coarse_ref, strided, sems):
    (copy,) = fetch(((coarse_hbm, coarse_ref),), sems)
    held, coarse = coarse_ref.shape
    blocks = coarse // LANES
    strided[...] = jnp.zeros_like(strided)
    copy.wait()
    for b in range(blocks):
        strided[pl.ds(b, held, stride=blocks), :] = coarse_ref[:, b * LANES : (b + 1) * LANES]
    lines_ref[...] = strided[: lines_ref.shape[0]].astype(BF)


def line_count(held, coarse):
    return -(-held * coarse // LANES // 16) * 16


def own_lines(coarse_inverse):
    count = line_count(*coarse_inverse.shape)
    return pl.pallas_call(
        lines_kernel,
        in_specs=[IN_HBM],
        out_shape=jax.ShapeDtypeStruct((count, LANES), BF),
        scratch_shapes=[
            pltpu.VMEM(coarse_inverse.shape, F32),
            pltpu.VMEM((2 * count, LANES), F32),
            pltpu.SemaphoreType.DMA((1,)),
        ],
        compiler_params=params(60),
    )(coarse_inverse)


def first_kernel(basis_hbm, orient_hbm, wide_ref, narrow_ref, basis_ref, orient_ref, sems):
    copies = fetch(((basis_hbm, basis_ref), (orient_hbm, orient_ref)), sems)
    for copy in copies:
        copy.wait()
    face = orient_ref.shape[1]
    for row, out in ((0, wide_ref), (1, narrow_ref)):
        order = one_hot(orient_ref[row : row + 1, :], face)
        part = padded(basis_ref[:, (2 + row) * face : (3 + row) * face])
        out[...] = dot_nt(part, order).astype(BF)


def first(basis, orient):
    shape = jax.ShapeDtypeStruct((SLOT, orient.shape[1]), BF)
    inputs = (basis, orient)
    return pl.pallas_call(
        first_kernel,
        in_specs=[IN_HBM] * len(inputs),
        out_shape=[shape, shape],
        scratch_shapes=[pltpu.VMEM(a.shape, a.dtype) for a in inputs] + [pltpu.SemaphoreType.DMA((len(inputs),))],
        compiler_params=params(60),
    )(*inputs)


def outgoing_kernel(res_ref, share_ref, face_wide_ref, face_narrow_ref):
    face = face_wide_ref.shape[1]
    given = res_ref[...].astype(F32) * (1.0 - share_ref[...].astype(F32))
    face_wide_ref[...] = given[:, :face].astype(BF)
    face_narrow_ref[...] = given[:, face:].astype(BF)


def outgoing(res, share):
    rows, owned_count = res.shape
    face = owned_count // 2
    block = rows // 3
    half = jax.ShapeDtypeStruct((rows, face), BF)
    by_rows = lambda i: (i, 0)
    return pl.pallas_call(
        outgoing_kernel,
        grid=(3,),
        in_specs=[pl.BlockSpec((block, owned_count), by_rows), whole(share.shape)],
        out_specs=[pl.BlockSpec((block, face), by_rows)] * 2,
        out_shape=[half, half],
        compiler_params=params(),
        cost_estimate=cost(40000 * res.size, 4 * res.size),
    )(res, share)


def stacked_bases(own_ref, wide_ref, narrow_ref):
    face = wide_ref.shape[1]
    zero = jnp.zeros((SLOT, face), BF)
    zeros = jnp.zeros((SLOT, 2 * face), BF)
    mine = jnp.concatenate([padded(own_ref[:, : 2 * face]), zeros, zeros, zeros], axis=0)
    theirs = jnp.concatenate(
        [
            zeros,
            jnp.concatenate([wide_ref[...], zero], axis=1),
            jnp.concatenate([zero, narrow_ref[...]], axis=1),
            zeros,
        ],
        axis=0,
    )
    return mine, theirs


def primal_kernel(res_ref, share_ref, own_ref, wide_ref, narrow_ref, out_ref):
    mine, theirs = stacked_bases(own_ref, wide_ref, narrow_ref)
    res = res_ref[...].astype(F32)
    shr = share_ref[...].astype(F32)
    kept = (res * shr).astype(BF)
    given = (res * (1.0 - shr)).astype(BF)
    out_ref[...] = (dot_nt(kept, mine) + dot_nt(given, theirs)).astype(BF)


def primal_parts(res, share, basis, basis_wide, basis_narrow):
    rows, owned_count = res.shape
    block = rows // 3
    return pl.pallas_call(
        primal_kernel,
        grid=(3,),
        in_specs=[
            pl.BlockSpec((block, owned_count), lambda i: (i, 0)),
            whole(share.shape),
            whole(basis.shape),
            whole(basis_wide.shape),
            whole(basis_narrow.shape),
        ],
        out_specs=pl.BlockSpec((block, LANES), lambda i: (i, 0)),
        out_shape=jax.ShapeDtypeStruct((rows, LANES), BF),
        compiler_params=params(60),
        cost_estimate=cost(4 * res.size * LANES, 2 * res.size),
    )(res, share, basis, basis_wide, basis_narrow)


def scatter_kernel(blocks, x_ref, high_ref, low_ref, out_ref, masked):
    rows = x_ref.shape[1]
    masked[...] = jnp.zeros_like(masked)
    total = jnp.zeros((blocks * SLOT, LANES), F32)
    for pair in range(x_ref.shape[0] // 2):
        x = jnp.concatenate([x_ref[2 * pair], x_ref[2 * pair + 1]], axis=1).astype(F32)
        high = jnp.concatenate([high_ref[2 * pair : 2 * pair + 1], high_ref[2 * pair + 1 : 2 * pair + 2]], axis=1)
        low = jnp.concatenate([low_ref[2 * pair : 2 * pair + 1], low_ref[2 * pair + 1 : 2 * pair + 2]], axis=1)
        x = jnp.concatenate([x, jnp.zeros((SLOT - rows, x.shape[1]), F32)], axis=0)
        for b in range(blocks):
            masked[b * SLOT : (b + 1) * SLOT] = jnp.where(high == b, x, 0.0).astype(BF)
        total += dot_nt(masked[...], one_hot(low, LANES))
    for b in range(blocks):
        out_ref[b] = total[b * SLOT : b * SLOT + rows].astype(BF)


def scatter(x, high, low, blocks):
    _, rows, _ = x.shape
    return pl.pallas_call(
        lambda *refs: scatter_kernel(blocks, *refs),
        out_shape=jax.ShapeDtypeStruct((blocks, rows, LANES), BF),
        scratch_shapes=[pltpu.VMEM((blocks * SLOT, 2 * LANES), BF)],
        compiler_params=params(),
    )(x, high, low)


def solve_kernel(parts_ref, *refs):
    *line_refs, out_ref, strided, inverse = refs
    parts, blocks, rows, _ = parts_ref.shape
    count = line_refs[0].shape[0]
    size = count // NZ
    strided[count:] = jnp.zeros((strided.shape[0] - count, LANES), F32)
    for x, ref in enumerate(line_refs):
        strided[:count] = ref[...].astype(F32)
        for z in range(NZ):
            at = x * LANES + z * 16
            for b in range(blocks):
                found = strided[pl.ds(z * size + b, 16, stride=blocks), :]
                inverse[at : at + 16, b * LANES : (b + 1) * LANES] = found.astype(BF)
    total = jnp.concatenate([sum(parts_ref[p, b].astype(F32) for p in range(parts)) for b in range(blocks)], axis=1)
    top = total.astype(BF)
    rest = (total - top.astype(F32)).astype(BF)
    both = jnp.concatenate([top.astype(F32), rest.astype(F32)], axis=0).astype(BF)
    product = dot_nt(both, inverse[...])
    product = (product[:rows] + product[rows:]).astype(BF)
    for p in range(NX):
        for n in range(out_ref.shape[0]):
            out_ref[n, p] = product[:, p * LANES : (p + 1) * LANES]


def solve(parts, lines):
    _, blocks, rows, _ = parts.shape
    spare = 16 * blocks
    return pl.pallas_call(
        solve_kernel,
        out_shape=jax.ShapeDtypeStruct((NARROW, NX, rows, LANES), BF),
        scratch_shapes=[
            pltpu.VMEM((lines[0].shape[0] + spare, LANES), F32),
            pltpu.VMEM((NX * LANES, blocks * LANES), BF),
        ],
        compiler_params=params(16),
        cost_estimate=cost(100_000_000_000, 4_000_000),
    )(parts, *lines)


def gather_kernel(rows, corr_ref, high_ref, low_ref, out_ref):
    blocks = corr_ref.shape[0] // rows
    for pair in range(out_ref.shape[0] // 2):
        high = jnp.concatenate([high_ref[2 * pair : 2 * pair + 1], high_ref[2 * pair + 1 : 2 * pair + 2]], axis=1)
        low = jnp.concatenate([low_ref[2 * pair : 2 * pair + 1], low_ref[2 * pair + 1 : 2 * pair + 2]], axis=1)
        found = jnp.dot(corr_ref[...], one_hot(low, LANES), preferred_element_type=F32)
        total = jnp.zeros((rows, 2 * LANES), F32)
        for b in range(blocks):
            total = jnp.where(high == b, found[b * rows : (b + 1) * rows], total)
        out_ref[2 * pair] = total[:, :LANES].astype(BF)
        out_ref[2 * pair + 1] = total[:, LANES:].astype(BF)


def gather(corr, high, low, rows):
    return pl.pallas_call(
        lambda *refs: gather_kernel(rows, *refs),
        out_shape=jax.ShapeDtypeStruct((high.shape[0], rows, LANES), BF),
        compiler_params=params(),
    )(corr, high, low)


def column_copies(inverse_hbm, inverse, sems, first_column):
    count, rows, width = inverse.shape
    return [
        pltpu.make_async_copy(
            inverse_hbm.at[pl.ds(0, rows), pl.ds((first_column + i) * width, width)], inverse.at[i], sems.at[i]
        )
        for i in range(count)
    ]


def faces_kernel(
    res_ref, share_ref, got_wide_ref, got_narrow_ref, orient_ref, inverse_hbm, gathered_ref, wide_ref, narrow_ref, inverse, sems
):
    face = orient_ref.shape[1]
    copies = column_copies(inverse_hbm, inverse, sems, 2)
    for copy in copies:
        copy.start()
    gathered_ref[:, : 2 * face] = (res_ref[...].astype(F32) * share_ref[...].astype(F32)).astype(BF)
    orders = [one_hot(orient_ref[row : row + 1, :], face) for row in (0, 1)]
    for row, ref in ((0, got_wide_ref), (1, got_narrow_ref)):
        found = jnp.dot(ref[...], orders[row], preferred_element_type=F32)
        gathered_ref[:, (2 + row) * face : (3 + row) * face] = found.astype(BF)
    for row, ref in ((0, wide_ref), (1, narrow_ref)):
        copies[row].wait()
        product = jnp.dot(gathered_ref[...], inverse[row], preferred_element_type=F32).astype(BF)
        ref[...] = dot_nt(product, orders[row]).astype(BF)


def faces(res, share, got_wide, got_narrow, orient, inverse):
    rows = res.shape[0]
    face = orient.shape[1]
    unknowns = inverse.shape[0]
    half = jax.ShapeDtypeStruct((rows, face), BF)
    inputs = (res, share, got_wide, got_narrow, orient)
    return pl.pallas_call(
        faces_kernel,
        in_specs=[pl.BlockSpec(memory_space=pltpu.VMEM)] * len(inputs) + [IN_HBM],
        out_shape=[jax.ShapeDtypeStruct((rows, unknowns), BF), half, half],
        scratch_shapes=[pltpu.VMEM((2, unknowns, face), BF), pltpu.SemaphoreType.DMA((2,))],
        compiler_params=params(56),
        cost_estimate=cost(4 * rows * face * unknowns + 8 * rows * face * face, 4 * face * unknowns + 8 * rows * face),
    )(*inputs, inverse)


def owned_kernel(gathered_ref, inverse_hbm, out_ref, inverse, sems):
    copies = column_copies(inverse_hbm, inverse, sems, 0)
    face = inverse.shape[2]
    for copy in copies:
        copy.start()
    for i, copy in enumerate(copies):
        copy.wait()
        product = jnp.dot(gathered_ref[...], inverse[i], preferred_element_type=F32)
        out_ref[:, i * face : (i + 1) * face] = product.astype(BF)


def owned(gathered, inverse, face):
    rows, unknowns = gathered.shape
    return pl.pallas_call(
        owned_kernel,
        in_specs=[pl.BlockSpec(memory_space=pltpu.VMEM), IN_HBM],
        out_shape=jax.ShapeDtypeStruct((rows, 2 * face), BF),
        scratch_shapes=[pltpu.VMEM((2, unknowns, face), BF), pltpu.SemaphoreType.DMA((2,))],
        compiler_params=params(56),
        cost_estimate=cost(4 * rows * face * unknowns, 4 * face * unknowns + 4 * rows * unknowns),
    )(gathered, inverse)


def final_kernel(local_ref, back_wide_ref, back_narrow_ref, corr_ref, share_ref, own_ref, wide_ref, narrow_ref, out_ref):
    mine, theirs = stacked_bases(own_ref, wide_ref, narrow_ref)
    shr = share_ref[...].astype(F32)
    corr = corr_ref[...]
    kept = local_ref[...].astype(F32) + jnp.dot(corr, mine, preferred_element_type=F32)
    back = jnp.concatenate([back_wide_ref[...], back_narrow_ref[...]], axis=1).astype(F32)
    back = back + jnp.dot(corr, theirs, preferred_element_type=F32)
    out_ref[0] = (shr * kept + (1.0 - shr) * back).astype(BF)


def final(local, back_wide, back_narrow, corr, share, basis, basis_wide, basis_narrow):
    rows, owned_count = local.shape
    face = owned_count // 2
    block = rows // 3
    by_rows = lambda i: (i, 0)
    return pl.pallas_call(
        final_kernel,
        grid=(3,),
        in_specs=[
            pl.BlockSpec((block, owned_count), by_rows),
            pl.BlockSpec((block, face), by_rows),
            pl.BlockSpec((block, face), by_rows),
            pl.BlockSpec((block, LANES), by_rows),
            whole(share.shape),
            whole(basis.shape),
            whole(basis_wide.shape),
            whole(basis_narrow.shape),
        ],
        out_specs=pl.BlockSpec((1, block, owned_count), lambda i: (0, i, 0)),
        out_shape=jax.ShapeDtypeStruct((1, rows, owned_count), BF),
        compiler_params=params(12),
    )(local, back_wide, back_narrow, corr, share, basis, basis_wide, basis_narrow)


def patch_columns(primal_index):
    narrow = lax.axis_index(NARROW_AXES)
    count = primal_index.shape[1]
    grid = primal_index.reshape(WIDE, NARROW, count)
    grid = jnp.pad(grid, ((0, 0), (0, 0), (0, SLOT - count)), constant_values=-1)
    own = lax.dynamic_index_in_dim(grid, narrow, 1, keepdims=False)
    beside = lax.dynamic_index_in_dim(grid, (narrow + 1) % NARROW, 1, keepdims=False)
    empty = jnp.full((WIDE, LANES - 3 * SLOT), -1, jnp.int32)
    return jnp.concatenate([own, jnp.roll(own, -1, axis=0), beside, empty], axis=1)


def held_place(columns, held):
    owner, row = columns // held, columns % held
    w, n = owner // NARROW, owner % NARROW
    by_x = (lax.axis_index("x") - w // NZ) % NX
    apart = (lax.axis_index("z") ^ w) % NZ
    by_z = apart // 4 + (apart // 2) % 2 * 2 + apart % 2 * 4
    return jnp.where(columns < 0, -1, n * NX + by_x), by_z * 16 + row


def on_device(residual, share, orient, local_inverse, primal_basis, primal_index, coarse_inverse):
    res = residual[0]
    ori = orient[0]
    inverse = local_inverse[0]
    basis = primal_basis[0]
    rows = res.shape[0]
    held, coarse = coarse_inverse.shape
    chunk = rows // WIDE

    lines = own_lines(coarse_inverse)
    other = exchange(lines, 4)
    mine_wide, mine_narrow = first(after(basis, lines), ori)
    basis_wide = shift(mine_wide, WIDE_AXES, -1)
    basis_narrow = shift(mine_narrow, NARROW_AXES, -1)
    lines = jnp.concatenate([lines, after(other, mine_wide)], axis=0)
    other = exchange(lines, 2)

    primal = primal_parts(after(res, lines), share, basis, basis_wide, basis_narrow)
    lines = jnp.concatenate([after(lines, primal), other], axis=0)
    other = exchange(lines, 1)
    chunks = lax.all_to_all(after(primal, lines).reshape(WIDE, chunk, LANES), WIDE_AXES, 0, 0)

    face_wide, face_narrow = outgoing(after(res, lines), share)
    got_narrow = shift(face_narrow, NARROW_AXES, 1)
    columns = patch_columns(after(primal_index, face_wide))
    high, low = columns >> 7, columns & 127
    high_held, low_held = held_place(columns, held)

    lines = jnp.concatenate([after(lines, high, high_held), other], axis=0)
    from_next = shift(lines, "x", -1)
    from_last = shift(lines, "x", 1)

    partial = scatter(after(chunks, lines), high, low, coarse // LANES)
    got_wide = shift(after(face_wide, partial), WIDE_AXES, 1)
    pieces = [lines, from_last, shift(from_next, "x", -1), from_next]
    parts = lax.all_gather(after(partial, from_next), NARROW_AXES)
    corr = solve(parts, pieces)

    gathered, send_wide, send_narrow = faces(res, share, after(got_wide, corr), got_narrow, ori, inverse)
    corr = lax.all_to_all(corr, NARROW_AXES, 0, 0)
    back_wide = shift(after(send_wide, corr), WIDE_AXES, -1)
    back_narrow = shift(after(send_narrow, corr), NARROW_AXES, -1)
    corr = gather(after(corr, send_wide).reshape(-1, LANES), high_held, low_held, chunk)
    local = owned(after(gathered, corr), inverse, face_wide.shape[1])
    corr = lax.all_to_all(corr, WIDE_AXES, 0, 0).reshape(rows, LANES)

    return final(local, back_wide, back_narrow, corr, share, basis, basis_wide, basis_narrow)


def solution(mesh):
    grid = jax.sharding.Mesh(mesh.devices.reshape(NX, NZ, NY, NCORE), WIDE_AXES + NARROW_AXES)
    patches = WIDE_AXES + NARROW_AXES
    placed = (
        P(patches, None, None),
        P(patches, None),
        P(patches, None, None),
        P(patches, None, None),
        P(patches, None, None),
        P(),
        P(patches, None),
    )
    return jax.shard_map(
        on_device,
        mesh=grid,
        in_specs=placed,
        out_specs=P(patches, None, None),
        check_vma=False,
    )
```
